32 devices in a mesh: seq: 8 (over y, x, core), head: 4 (over z).
Axes of the slice: x: 2, y: 2, z: 4, core: 2. Of those that a mesh axis runs over, the one named last changes fastest.
Arguments:
- hidden: bfloat16 [12288, 4096], P('seq', 'head'), may hold values from -6 to 6
- norm_gain: float32 [4096], replicated, may hold values from 0.1 to 1.9
- w_query: bfloat16 [4096, 4096], P(None, 'head'), may hold values from -0.09375 to 0.09375
- w_out: bfloat16 [4096, 4096], P('head'), may hold values from -0.5 to 0.5
- keys: bfloat16 [12288, 1024], P('seq', 'head'), may hold values from -240 to 240
- values: bfloat16 [12288, 1024], P('seq', 'head'), may hold values from -6 to 6
- cand_count: int32 [8], P('seq'), may hold values from 1 to 384, 768 in all
- cand_pos: int32 [3072], P('seq'), may hold values from 0 to 1535, as said below
Outputs:
- slot_update: bfloat16 [3072, 4096], P('seq', 'head')
The draws below stay inside these ranges and needn't reach their ends.
Inputs may be any that keep to these rules, and one draw needn't show every extreme that they name: `cand_pos`: each shard's 384 slots hold distinct positions within that shard; its first cand_count slots are the used ones. `cand_count`: the counts sum to 768.
All inputs are finite; a program needn't handle non-finite values. No bound on the sum of `cand_count` on one device may be relied on, other than what follows from the above.
Results may differ from the reference program's by a relative error of at most 0.019.
The reference program's roundings to bfloat16 on the way count: a program that leaves them out, or rounds other values in their place, can miss the bound.
Values may be sent and summed in bfloat16 or wider, within the bound.
A program may use at most 128 MiB of HBM per device.

```python
import math
import jax
import jax.numpy as jnp
import numpy as np
from jax import lax

D = 4096
QUERY_HEADS = 32
KEY_VALUE_HEADS = 8
HEAD_SIZE = 128
SEQ_DEV = 1536
CAP = 384
ROUTED_TOTAL = 768
SEQUENCE_TOKENS = 12288
N_SEQ = 8


def draw_keys(key, part):
    base_offset = 2.5 * jnp.clip(jax.random.normal(key, (SEQUENCE_TOKENS, KEY_VALUE_HEADS * HEAD_SIZE), jnp.float32), -6.0, 6.0)
    return base_offset.astype(jnp.bfloat16)


def draw_cand_pos(key, part):
    subkeys = jax.random.split(key, N_SEQ)

    def pick_slots(subkey):
        return jax.random.permutation(subkey, SEQ_DEV)[:CAP]
    picked = jax.vmap(pick_slots)(subkeys)
    return picked.reshape(N_SEQ * CAP).astype(jnp.int32)


def block_scale(key, shape, shards, least, high):
    def one(dim, shards_of):
        draws = jax.random.uniform(jax.random.fold_in(jax.random.fold_in(key, 6), dim), (shards_of,), jnp.float32, least / len(shards), high / len(shards))
        return jnp.repeat(jnp.exp(draws), shape[dim] // shards_of).reshape((-1,) + (1,) * (len(shape) - dim - 1))

    gain = one(*shards[0])
    for cut in shards[1:]:
        gain = gain * one(*cut)
    return gain


def split_up(number_of, total, bound, slope):
    weights = [(1 << 20) // math.isqrt(grade ** slope) + 1 for grade in range(2, number_of + 1)]
    spare, counts = total - bound - (number_of - 1), [1] * (number_of - 1)
    while spare > 0:
        movable = [i for i in range(number_of - 1) if counts[i] < bound]
        pool, remaining = sum([weights[i] for i in movable]), spare
        for i in movable:
            addition = min(bound - counts[i], max(1, remaining * weights[i] // pool), spare)
            counts[i] = counts[i] + addition
            spare = spare - addition
    return np.array([bound] + counts)


def ragged(rng, count, total, reach, skew):
    if count == 2:
        one = jax.random.randint(rng, (), max(1, total - reach), min(reach, total - 1) + 1)
        return jnp.stack([one, total - one])
    sizes = jnp.asarray(split_up(count, total, reach, skew), jnp.int32)
    couples = (count - 1) // 2
    source_of, taker = sizes[1:1 + 2 * couples:2], sizes[2:2 + 2 * couples:2]
    room = jnp.minimum(source_of - 1, reach - taker)
    shifted = jax.random.randint(jax.random.fold_in(rng, 1), (couples,), 0, 1 << 20) % (room + 1)
    sizes = sizes.at[1:1 + 2 * couples:2].set(source_of - shifted).at[2:2 + 2 * couples:2].set(taker + shifted)
    return sizes[jax.random.permutation(jax.random.fold_in(rng, 2), count)]


def gaussian(stream_key, dims, scale, most, pieces=(), held_as=jnp.bfloat16):
    array = jax.random.normal(stream_key, dims, jnp.float32) * scale
    if len(pieces) > 0:
        array = block_scale(stream_key, dims, pieces, -0.22, 0.18) * array
    return jnp.clip(array, min=-most, max=most).astype(held_as)


def setup_inputs(seed: int = 0) -> dict:
    streams_of = jax.random.split(jax.random.key(seed), 9)
    hidden = gaussian(streams_of[0], (SEQUENCE_TOKENS, D), 1.0, 6.0, ((0, 8), (1, 4)))
    norm_gain = jnp.clip(1.0 + 0.18 * jax.random.normal(streams_of[1], (D,), jnp.float32), 0.1, 1.9)
    w_query = gaussian(streams_of[2], (D, QUERY_HEADS * HEAD_SIZE), D ** -0.5, 0.09375, ((1, 4),))
    w_out = gaussian(streams_of[3], (QUERY_HEADS * HEAD_SIZE, D), HEAD_SIZE ** -0.5, 0.5, ((0, 4),))
    keys = draw_keys(jax.random.fold_in(streams_of[8], 71), 0)
    values = gaussian(streams_of[5], (SEQUENCE_TOKENS, KEY_VALUE_HEADS * HEAD_SIZE), 1.0, 6.0, ((0, 8), (1, 4)))
    cand_count = ragged(streams_of[6], N_SEQ, ROUTED_TOTAL, CAP, 2).astype(jnp.int32)
    cand_pos = draw_cand_pos(jax.random.fold_in(streams_of[8], 71), 0)
    return {"hidden": hidden, "norm_gain": norm_gain, "w_query": w_query, "w_out": w_out, "keys": keys, "values": values, "cand_count": cand_count, "cand_pos": cand_pos}


EPS = 1e-05
ROPE_BASE = 500000.0

def rotate(query_rows, positions):
    half_dim = HEAD_SIZE // 2
    inverse_freq = jnp.exp(-math.log(ROPE_BASE) * 2.0 * jnp.arange(half_dim, dtype=jnp.float32) / HEAD_SIZE)
    angles = positions.astype(jnp.float32)[:, None] * inverse_freq[None, :]
    cosine = jnp.cos(angles)[:, None, :]
    sine_part = jnp.sin(angles)[:, None, :]
    first_half = query_rows[..., :half_dim]
    second_half = query_rows[..., half_dim:]
    return jnp.concatenate([first_half * cosine - second_half * sine_part, second_half * cosine + first_half * sine_part], axis=-1)

def reference(hidden, norm_gain, w_query, w_out, keys, values, cand_count, cand_pos):
    slot_ids = jnp.arange(N_SEQ * CAP, dtype=jnp.int32)
    owner_shard = slot_ids // CAP
    within = slot_ids % CAP
    offsets = (jnp.cumsum(cand_count) - cand_count).astype(jnp.int32)
    is_live = within < cand_count[owner_shard]
    row_ids = jnp.where(is_live, offsets[owner_shard] + within, ROUTED_TOTAL).astype(jnp.int32)
    positions = (owner_shard * SEQ_DEV + cand_pos).astype(jnp.int32)
    compact_pos = jnp.zeros((ROUTED_TOTAL + 1,), jnp.int32).at[row_ids].set(positions)[:ROUTED_TOTAL]
    gathered = hidden[compact_pos].astype(jnp.float32)
    inv_rms = lax.rsqrt(lax.optimization_barrier(jnp.mean(gathered * gathered, axis=1, keepdims=True)) + EPS)
    normed = (gathered * inv_rms * norm_gain).astype(jnp.bfloat16)
    query_rows = jnp.dot(normed, w_query, preferred_element_type=jnp.float32).reshape(ROUTED_TOTAL, QUERY_HEADS, HEAD_SIZE)
    query_rows = (rotate(query_rows, compact_pos) * (1.0 / math.sqrt(HEAD_SIZE))).astype(jnp.bfloat16)
    rows_per_block = 32
    grouped_heads = query_rows.reshape(ROUTED_TOTAL // rows_per_block, rows_per_block, KEY_VALUE_HEADS, QUERY_HEADS // KEY_VALUE_HEADS, HEAD_SIZE)
    key_widened = keys.reshape(SEQUENCE_TOKENS, KEY_VALUE_HEADS, HEAD_SIZE).astype(jnp.float32)
    value_widened = values.reshape(SEQUENCE_TOKENS, KEY_VALUE_HEADS, HEAD_SIZE).astype(jnp.float32)
    key_index = jnp.arange(SEQUENCE_TOKENS, dtype=jnp.int32)

    def attend(block_item):
        block_q, block_pos = block_item
        scores = jnp.einsum('qgrd,tgd->qgrt', block_q.astype(jnp.float32), key_widened)
        visible = key_index[None, None, None, :] <= block_pos[:, None, None, None]
        scores = jnp.where(visible, scores, -jnp.inf)
        peak_row = lax.optimization_barrier(jnp.max(scores, axis=3, keepdims=True))
        weight = jnp.exp(scores - peak_row)
        denominator = lax.optimization_barrier(jnp.sum(weight, axis=3))
        rounded = lax.optimization_barrier(weight.astype(jnp.bfloat16))
        numerator = jnp.einsum('qgrt,tgd->qgrd', rounded.astype(jnp.float32), value_widened)
        return (numerator / denominator[..., None]).astype(jnp.bfloat16)
    mixed_heads = lax.map(attend, (grouped_heads, compact_pos.reshape(ROUTED_TOTAL // rows_per_block, rows_per_block)))
    mixed_heads = mixed_heads.reshape(ROUTED_TOTAL, QUERY_HEADS * HEAD_SIZE)
    update = jnp.dot(mixed_heads, w_out, preferred_element_type=jnp.float32).astype(jnp.bfloat16)
    padded = jnp.concatenate([update, jnp.zeros((1, D), jnp.bfloat16)], axis=0)
    return padded[row_ids]
```

```python
import functools
import math

import jax
import jax.numpy as jnp
from jax import lax
from jax.experimental import pallas as pl
from jax.experimental.pallas import tpu as pltpu
from jax.sharding import PartitionSpec as P

HEAD_SIZE = 128
M_DEV = 96
LANES = 128
TILE = 256

EPS = 1e-05
ROPE_BASE = 500000.0
NEG_FLOOR = -1e30
MESH = pl.DeviceIdType.MESH
F32 = jnp.float32
BF16 = jnp.bfloat16
I32 = jnp.int32


def iota(shape, dim):
    return lax.broadcasted_iota(I32, shape, dim)


def flip_bits(index, step, count):
    out, bit = 0, 1
    while bit < count:
        out = out + bit * (((index // bit) % 2 + (step // bit) % 2) % 2)
        bit *= 2
    return out


def kernel(
    n, nh, bucket,
    meta_ref, hidden_ref, gain_ref, wq_ref, wo_ref, key_ref, val_ref,
    out_ref,
    hid, wq, wo, kbuf, vbuf, vext,
    meta_all, onehot, send_rows, recv_rows, feats, normed, q_all,
    o_send, ml_send, o_recv, ml_recv, mixed, part_send, part_recv, upd, back_send, back_recv,
    load_sem, meta_s, meta_r, rows_s, rows_r, feat_s, feat_r, q_s, q_r,
    o_s, o_r, ml_s, ml_r, part_s, part_r, back_s, back_r,
):
    seq_dev, width = hid.shape
    slots = meta_ref.shape[1] - LANES
    kv_local = key_ref.shape[1] // HEAD_SIZE
    q_cols = wq.shape[1]
    q_local = q_cols // HEAD_SIZE
    repeat = q_local // kv_local
    shift = int(math.log2(n))
    entries = n * bucket
    me = lax.axis_index("seq")
    hme = lax.axis_index("head")

    def load(i, src, dst):
        return pltpu.make_async_copy(src, dst, load_sem.at[i])

    loads = [
        load(0, hidden_ref, hid), load(1, wq_ref, wq), load(2, key_ref, kbuf),
        load(3, val_ref, vbuf), load(4, wo_ref, wo),
    ]
    for copy in loads:
        copy.start()

    barrier = pltpu.get_barrier_semaphore()
    for step in range(1, n):
        pl.semaphore_signal(
            barrier, inc=1, device_id=(flip_bits(me, step, n), hme), device_id_type=MESH
        )
    for step in range(1, nh):
        pl.semaphore_signal(
            barrier, inc=1, device_id=(me, (hme + step) % nh), device_id_type=MESH
        )
    pl.semaphore_wait(barrier, n - 1 + nh - 1)

    def to_seq(src, dst, send, recv, peer):
        return pltpu.make_async_remote_copy(
            src_ref=src, dst_ref=dst.at[me], send_sem=send.at[peer], recv_sem=recv.at[me],
            device_id=(peer, hme), device_id_type=MESH,
        )

    def from_seq(src, dst, send, recv, peer):
        return pltpu.make_async_remote_copy(
            src_ref=src, dst_ref=dst.at[peer], send_sem=send.at[peer], recv_sem=recv.at[peer],
            device_id=(peer, hme), device_id_type=MESH,
        )

    def to_head(src, dst, send, recv, peer):
        return pltpu.make_async_remote_copy(
            src_ref=src, dst_ref=dst.at[hme], send_sem=send.at[peer], recv_sem=recv.at[hme],
            device_id=(me, peer), device_id_type=MESH,
        )

    def from_head(src, dst, send, recv, peer):
        return pltpu.make_async_remote_copy(
            src_ref=src, dst_ref=dst.at[peer], send_sem=send.at[peer], recv_sem=recv.at[peer],
            device_id=(me, peer), device_id_type=MESH,
        )

    peers = [flip_bits(me, step, n) for step in range(1, n)]
    heads = [(hme + step) % nh for step in range(1, nh)]
    for peer in peers:
        to_seq(meta_ref, meta_all, meta_s, meta_r, peer).start()
    meta_all[me] = meta_ref[...]
    for peer in peers:
        from_seq(meta_ref, meta_all, meta_s, meta_r, peer).wait_recv()

    counts = [meta_all[s, 0:1, slots : slots + 1] for s in range(n)]
    offs, total = [], jnp.zeros((1, 1), I32)
    my_off = jnp.zeros((1, 1), I32)
    my_count = meta_ref[0:1, slots : slots + 1]
    for s in range(n):
        offs.append(total)
        my_off = my_off + counts[s] * jnp.where(me > s, 1, 0)
        total = total + counts[s]

    loads[0].wait()
    my_pos = meta_ref[0:1, 0:slots]
    for d in range(n):
        slot = iota((bucket, slots), 0) * n + ((d - my_off) & (n - 1))
        at = jnp.where(iota((bucket, slots), 1) == slot, my_pos, 0).astype(F32)
        place = jnp.sum(at, axis=1, keepdims=True)
        token = iota((bucket, seq_dev), 1).astype(F32)
        onehot[d * bucket : (d + 1) * bucket, :] = jnp.where(token == place, 1.0, 0.0).astype(BF16)

    def pick(t, _):
        cols = pl.ds(pl.multiple_of(t * TILE, TILE), TILE)
        rows = jnp.dot(onehot[...], hid[:, cols], preferred_element_type=F32)
        send_rows[:, :, cols] = rows.astype(BF16).reshape(n, bucket, TILE)
        return 0

    lax.fori_loop(0, width // TILE, pick, 0)
    for peer in peers:
        to_seq(send_rows.at[peer], recv_rows, rows_s, rows_r, peer).start()
    recv_rows[me] = send_rows[me]

    def bucket_of(s, d):
        first = (d - offs[s]) & (n - 1)
        return (offs[s] + first) >> shift, first

    row_m = iota((M_DEV, entries), 0)
    lane_e = iota((M_DEV, entries), 1)
    placing = jnp.zeros((M_DEV, entries), F32)
    for s in range(n):
        base, first = bucket_of(s, me)
        k = lane_e - s * bucket
        hit = (k >= 0) & (k < bucket) & (row_m == base + k) & (k * n + first < counts[s])
        placing = jnp.where(hit, 1.0, placing)
    placing = placing.astype(BF16)

    def positions(d):
        row = iota((M_DEV, slots), 0) * n + d
        lane = iota((M_DEV, slots), 1)
        found = jnp.zeros((M_DEV, slots), I32)
        for s in range(n):
            hit = (lane + offs[s] == row) & (lane < counts[s])
            found = jnp.where(hit, meta_all[s, 0:1, 0:slots] + s * seq_dev, found)
        return jnp.sum(found.astype(F32), axis=1, keepdims=True)

    lane = iota((M_DEV, LANES), 1)
    half = HEAD_SIZE // 2
    freq = jnp.exp(
        (-math.log(ROPE_BASE) * 2.0 / HEAD_SIZE) * (lane % half).astype(F32)
    )
    angle = positions(me) * freq
    cosine = jnp.cos(angle)
    sine = jnp.where(lane < half, -jnp.sin(angle), jnp.sin(angle))
    loads[3].wait()
    for g in range(kv_local):
        vext[g, :, 0:HEAD_SIZE] = vbuf[:, g * HEAD_SIZE : (g + 1) * HEAD_SIZE]
        vext[g, :, HEAD_SIZE : 2 * HEAD_SIZE] = jnp.ones((seq_dev, HEAD_SIZE), BF16)

    for peer in peers:
        from_seq(send_rows.at[peer], recv_rows, rows_s, rows_r, peer).wait_recv()
    gathered = recv_rows[...].reshape(entries, width)
    feats[hme] = jnp.dot(placing, gathered, preferred_element_type=F32).astype(BF16)

    for peer in heads:
        to_head(feats.at[hme], feats, feat_s, feat_r, peer).start()
    for peer in heads:
        from_head(feats.at[hme], feats, feat_s, feat_r, peer).wait_recv()
    square = jnp.zeros((M_DEV, 1), F32)
    for h in range(nh):
        wide = feats[h].astype(F32)
        square = square + jnp.sum(wide * wide, axis=1, keepdims=True)
    inv_rms = lax.rsqrt(square * (1.0 / (nh * width)) + EPS)
    for h in range(nh):
        gain = gain_ref[0:1, h * width : (h + 1) * width]
        normed[:, h * width : (h + 1) * width] = (
            feats[h].astype(F32) * inv_rms * gain
        ).astype(BF16)

    loads[1].wait()
    scale = 1.0 / math.sqrt(HEAD_SIZE)

    def project(t, _):
        cols = pl.ds(pl.multiple_of(t * TILE, TILE), TILE)
        raw = jnp.dot(normed[...], wq[:, cols], preferred_element_type=F32)
        turned = []
        for i in range(TILE // HEAD_SIZE):
            one = raw[:, i * HEAD_SIZE : (i + 1) * HEAD_SIZE]
            turned.append((one * cosine + pltpu.roll(one, half, 1) * sine) * scale)
        q_all[me, :, cols] = jnp.concatenate(turned, axis=1).astype(BF16)
        return 0

    lax.fori_loop(0, q_cols // TILE, project, 0)
    for peer in peers:
        to_seq(q_all.at[me], q_all, q_s, q_r, peer).start()
    loads[2].wait()

    token = me * seq_dev + iota((1, seq_dev), 1)
    token = token.astype(F32)

    def attend(step, _):
        d = flip_bits(me, step, n)

        pos = positions(d)

        @pl.when(step > 0)
        def _():
            from_seq(q_all.at[me], q_all, q_s, q_r, d).wait_recv()

        hidden_bias = jnp.concatenate([pos] * repeat, axis=0)
        stats = jnp.zeros((M_DEV, LANES), F32)
        for g in range(kv_local):
            rows = jnp.concatenate(
                [
                    q_all[d, :, (g * repeat + i) * HEAD_SIZE : (g * repeat + i + 1) * HEAD_SIZE]
                    for i in range(repeat)
                ],
                axis=0,
            )
            score = lax.dot_general(
                rows, kbuf[:, g * HEAD_SIZE : (g + 1) * HEAD_SIZE],
                (((1,), (1,)), ((), ())), preferred_element_type=F32,
            )
            score = jnp.where(token <= hidden_bias, score, NEG_FLOOR)
            peak = jnp.max(score, axis=1, keepdims=True)
            weight = jnp.exp(score - peak).astype(BF16)
            both = jnp.dot(weight, vext[g], preferred_element_type=F32)
            for i in range(repeat):
                head = g * repeat + i
                part = slice(i * M_DEV, (i + 1) * M_DEV)
                o_send[d, :, head * HEAD_SIZE : (head + 1) * HEAD_SIZE] = (
                    both[part, 0:HEAD_SIZE].astype(BF16)
                )
                stats = jnp.where(lane == head, peak[part], stats)
                stats = jnp.where(lane == q_local + head, both[part, HEAD_SIZE:], stats)
        ml_send[d] = stats

        @pl.when(step > 0)
        def _():
            to_seq(o_send.at[d], o_recv, o_s, o_r, d).start()
            to_seq(ml_send.at[d], ml_recv, ml_s, ml_r, d).start()

        return 0

    lax.fori_loop(0, n, attend, 0)
    o_recv[me] = o_send[me]
    ml_recv[me] = ml_send[me]
    for peer in peers:
        from_seq(ml_send.at[peer], ml_recv, ml_s, ml_r, peer).wait_recv()
        from_seq(o_send.at[peer], o_recv, o_s, o_r, peer).wait_recv()

    top = ml_recv[0]
    for s in range(1, n):
        top = jnp.maximum(top, ml_recv[s])
    denom = jnp.zeros((M_DEV, LANES), F32)
    for s in range(n):
        aligned = pltpu.roll(ml_recv[s], LANES - q_local, 1)
        denom = denom + jnp.exp(ml_recv[s] - top) * aligned
    factor = [jnp.exp(ml_recv[s] - top) / denom for s in range(n)]
    for head in range(q_local):
        cols = slice(head * HEAD_SIZE, (head + 1) * HEAD_SIZE)
        joined = jnp.zeros((M_DEV, HEAD_SIZE), F32)
        for s in range(n):
            joined = joined + factor[s][:, head : head + 1] * o_recv[s, :, cols].astype(F32)
        mixed[:, cols] = joined.astype(BF16)

    loads[4].wait()
    for peer in heads + [hme]:

        def block(t, _):
            cols = pl.ds(pl.multiple_of(t * TILE, TILE), TILE)
            src = pl.ds(pl.multiple_of(peer * width + t * TILE, TILE), TILE)
            part_send[peer, :, cols] = jnp.dot(
                mixed[...], wo[:, src], preferred_element_type=F32
            ).astype(BF16)
            return 0

        lax.fori_loop(0, width // TILE, block, 0)
        if peer is not hme:
            to_head(part_send.at[peer], part_recv, part_s, part_r, peer).start()
    part_recv[hme] = part_send[hme]
    for peer in heads:
        from_head(part_send.at[peer], part_recv, part_s, part_r, peer).wait_recv()
    update = part_recv[0].astype(F32)
    for h in range(1, nh):
        update = update + part_recv[h].astype(F32)
    upd[0:M_DEV, :] = update.astype(BF16)
    upd[M_DEV:, :] = jnp.zeros((upd.shape[0] - M_DEV, width), BF16)

    for s in range(n):
        base, first = bucket_of(s, me)
        k = iota((bucket, LANES), 0)
        hit = (iota((bucket, LANES), 1) == base + k) & (k * n + first < counts[s])
        onehot[s * bucket : (s + 1) * bucket, 0:LANES] = jnp.where(hit, 1.0, 0.0).astype(BF16)
    back = jnp.dot(onehot[:, 0:LANES], upd[...], preferred_element_type=F32)
    back_send[...] = back.astype(BF16).reshape(n, bucket, width)
    for peer in peers:
        to_seq(back_send.at[peer], back_recv, back_s, back_r, peer).start()
    back_recv[me] = back_send[me]
    slot = iota((slots, entries), 0)
    entry = ((slot + my_off) & (n - 1)) * bucket + (slot >> shift)
    hit = (iota((slots, entries), 1) == entry) & (slot < my_count)
    restoring = jnp.where(hit, 1.0, 0.0).astype(BF16)
    for peer in peers:
        from_seq(back_send.at[peer], back_recv, back_s, back_r, peer).wait_recv()
    out_ref[...] = jnp.dot(
        restoring, back_recv[...].reshape(entries, width), preferred_element_type=F32
    ).astype(BF16)

    for peer in peers:
        to_seq(meta_ref, meta_all, meta_s, meta_r, peer).wait_send()
        to_seq(send_rows.at[peer], recv_rows, rows_s, rows_r, peer).wait_send()
        to_seq(q_all.at[me], q_all, q_s, q_r, peer).wait_send()
        to_seq(o_send.at[peer], o_recv, o_s, o_r, peer).wait_send()
        to_seq(ml_send.at[peer], ml_recv, ml_s, ml_r, peer).wait_send()
        to_seq(back_send.at[peer], back_recv, back_s, back_r, peer).wait_send()
    for peer in heads:
        to_head(feats.at[hme], feats, feat_s, feat_r, peer).wait_send()
        to_head(part_send.at[peer], part_recv, part_s, part_r, peer).wait_send()


def body(hidden, norm_gain, w_query, w_out, keys, values, cand_count, cand_pos):
    n, nh = lax.axis_size("seq"), lax.axis_size("head")
    seq_dev, width = hidden.shape
    slots = cand_pos.shape[0]
    bucket = -(-slots // n)
    bucket = -(-bucket // 16) * 16
    entries = n * bucket
    q_cols = w_query.shape[1]
    kv_local = keys.shape[1] // HEAD_SIZE
    meta = jnp.concatenate([cand_pos, jnp.broadcast_to(cand_count, (LANES,))])
    meta = jnp.broadcast_to(meta[None, :], (8, slots + LANES))
    seq_sem, head_sem = pltpu.SemaphoreType.DMA((n,)), pltpu.SemaphoreType.DMA((nh,))
    vmem, hbm = pl.BlockSpec(memory_space=pltpu.VMEM), pl.BlockSpec(memory_space=pl.ANY)
    return pl.pallas_call(
        functools.partial(kernel, n, nh, bucket),
        out_shape=jax.ShapeDtypeStruct((slots, width), BF16),
        in_specs=[vmem, hbm, vmem, hbm, hbm, hbm, hbm],
        out_specs=vmem,
        scratch_shapes=[
            pltpu.VMEM(hidden.shape, BF16),
            pltpu.VMEM(w_query.shape, BF16),
            pltpu.VMEM(w_out.shape, BF16),
            pltpu.VMEM(keys.shape, BF16),
            pltpu.VMEM(values.shape, BF16),
            pltpu.VMEM((kv_local, seq_dev, 2 * HEAD_SIZE), BF16),
            pltpu.VMEM((n, 8, slots + LANES), I32),
            pltpu.VMEM((entries, seq_dev), BF16),
            pltpu.VMEM((n, bucket, width), BF16),
            pltpu.VMEM((n, bucket, width), BF16),
            pltpu.VMEM((nh, M_DEV, width), BF16),
            pltpu.VMEM((M_DEV, nh * width), BF16),
            pltpu.VMEM((n, M_DEV, q_cols), BF16),
            pltpu.VMEM((n, M_DEV, q_cols), BF16),
            pltpu.VMEM((n, M_DEV, LANES), F32),
            pltpu.VMEM((n, M_DEV, q_cols), BF16),
            pltpu.VMEM((n, M_DEV, LANES), F32),
            pltpu.VMEM((M_DEV, q_cols), BF16),
            pltpu.VMEM((nh, M_DEV, width), BF16),
            pltpu.VMEM((nh, M_DEV, width), BF16),
            pltpu.VMEM((LANES, width), BF16),
            pltpu.VMEM((n, bucket, width), BF16),
            pltpu.VMEM((n, bucket, width), BF16),
            pltpu.SemaphoreType.DMA((5,)),
            seq_sem, seq_sem, seq_sem, seq_sem, head_sem, head_sem, seq_sem, seq_sem,
            seq_sem, seq_sem, seq_sem, seq_sem, head_sem, head_sem, seq_sem, seq_sem,
        ],
        compiler_params=pltpu.CompilerParams(
            collective_id=0, has_side_effects=True, vmem_limit_bytes=60 * 1024 * 1024
        ),
        name="routed_attention",
    )(meta, hidden, norm_gain[None, :], w_query, w_out, keys, values)


def solution(mesh):
    in_specs = (
        P("seq", "head"),
        P(),
        P(None, "head"),
        P("head", None),
        P("seq", "head"),
        P("seq", "head"),
        P("seq"),
        P("seq"),
    )
    out_specs = P("seq", "head")
    return jax.shard_map(body, mesh=mesh, in_specs=in_specs, out_specs=out_specs, check_vma=False)
```

```python
import functools
import math

import jax
import jax.numpy as jnp
from jax import lax
from jax.experimental import pallas as pl
from jax.experimental.pallas import tpu as pltpu
from jax.sharding import PartitionSpec as P

HEAD_SIZE = 128
M_DEV = 96
CHUNKS = 3
LANES = 128
TILE = 256

EPS = 1e-05
ROPE_BASE = 500000.0
NEG_FLOOR = -1e30
MESH = pl.DeviceIdType.MESH
F32 = jnp.float32
BF16 = jnp.bfloat16
I32 = jnp.int32


def iota(shape, dim):
    return lax.broadcasted_iota(I32, shape, dim)


def flip_bits(index, step, count):
    out, bit = 0, 1
    while bit < count:
        out = out + bit * (((index // bit) % 2 + (step // bit) % 2) % 2)
        bit *= 2
    return out


def kernel(
    n, nh, bucket,
    pos_ref, count_ref, hidden_ref, gain_ref, wq_ref, wo_ref, key_ref, val_ref,
    out_ref,
    hid, wq, wo, kbuf, vbuf, vext,
    meta, meta_all, onehot, send_rows, recv_rows, feats, normed, q_all,
    o_send, ml_send, o_recv, ml_recv, mixed, part_send, part_recv, upd, back_send, back_recv,
    load_sem, meta_s, meta_r, rows_s, rows_r, feat_s, feat_r, q_s, q_r, pass_s,
    o_s, o_r, ml_s, ml_r, part_s, part_r, back_s, back_r,
):
    seq_dev, width = hid.shape
    slots = pos_ref.shape[1]
    kv_local = key_ref.shape[1] // HEAD_SIZE
    q_cols = wq.shape[1]
    q_local = q_cols // HEAD_SIZE
    repeat = q_local // kv_local
    group = n * CHUNKS
    rows_c = M_DEV // CHUNKS
    per_chunk = n * bucket
    entries = CHUNKS * per_chunk
    low, bits = bucket - 1, int(math.log2(bucket))
    pairs = n // 2
    me = lax.axis_index("seq")
    hme = lax.axis_index("head")

    def load(i, src, dst):
        return pltpu.make_async_copy(src, dst, load_sem.at[i])

    loads = [
        load(0, hidden_ref, hid), load(1, val_ref, vbuf), load(2, wq_ref, wq),
        load(3, key_ref, kbuf), load(4, wo_ref, wo),
    ]
    loads[0].start()

    barrier = pltpu.get_barrier_semaphore()
    for step in range(1, n):
        pl.semaphore_signal(
            barrier, inc=1, device_id=(flip_bits(me, step, n), hme), device_id_type=MESH
        )
    for step in range(1, nh):
        pl.semaphore_signal(
            barrier, inc=1, device_id=(me, (hme + step) % nh), device_id_type=MESH
        )
    meta[:, 0:slots] = jnp.broadcast_to(pos_ref[...], (8, slots))
    meta[:, slots:] = jnp.broadcast_to(count_ref[...], (8, LANES))
    pl.semaphore_wait(barrier, n - 1 + nh - 1)

    def seq_copy(src, dst, send, recv, peer):
        return pltpu.make_async_remote_copy(
            src_ref=src, dst_ref=dst, send_sem=send, recv_sem=recv,
            device_id=(peer, hme), device_id_type=MESH,
        )

    def head_copy(src, dst, send, recv, peer):
        return pltpu.make_async_remote_copy(
            src_ref=src, dst_ref=dst, send_sem=send, recv_sem=recv,
            device_id=(me, peer), device_id_type=MESH,
        )

    def meta_copy(peer, slot):
        return seq_copy(meta, meta_all.at[slot], meta_s.at[peer], meta_r.at[slot], peer)

    def rows_copy(c, peer, slot):
        return seq_copy(
            send_rows.at[c, peer], recv_rows.at[c, slot], rows_s.at[c, peer],
            rows_r.at[c, slot], peer,
        )

    def feat_copy(c, peer, slot):
        return head_copy(
            feats.at[c, hme], feats.at[c, slot], feat_s.at[c, peer], feat_r.at[c, slot], peer
        )

    def q_copy(c, peer, slot):
        return seq_copy(
            q_all.at[c, me], q_all.at[c, slot], q_s.at[c, peer], q_r.at[c, slot], peer
        )

    def pass_copy(c, slot):
        return seq_copy(
            q_all.at[c, slot], q_all.at[c, slot], pass_s.at[c, slot], q_r.at[c, slot], sibling
        )

    def o_copy(c, peer, slot):
        return seq_copy(
            o_send.at[c, peer], o_recv.at[c, slot], o_s.at[c, peer], o_r.at[c, slot], peer
        )

    def ml_copy(c, peer, slot):
        return seq_copy(
            ml_send.at[c, peer], ml_recv.at[c, slot], ml_s.at[c, peer], ml_r.at[c, slot], peer
        )

    def part_copy(c, peer, slot):
        return head_copy(
            part_send.at[c, peer], part_recv.at[c, slot], part_s.at[c, peer],
            part_r.at[c, slot], peer,
        )

    def back_copy(c, peer, slot):
        return seq_copy(
            back_send.at[c, peer], back_recv.at[c, slot], back_s.at[c, peer],
            back_r.at[c, slot], peer,
        )

    sibling = flip_bits(me, 1, n)
    peers = [flip_bits(me, step, n) for step in range(n - 1, 0, -1)]
    cores = [flip_bits(me, step, n) for step in range(n - 2, 0, -2)]
    heads = [(hme + step) % nh for step in range(1, nh)]

    for peer in peers:
        meta_copy(peer, me).start()
    meta_all[me] = meta[...]
    loads[0].wait()
    for copy in loads[1:]:
        copy.start()
    upd[...] = jnp.zeros(upd.shape, BF16)
    for peer in peers:
        meta_copy(peer, peer).wait_recv()

    counts = [meta_all[s, 0:1, slots : slots + 1] for s in range(n)]
    offs, total = [], jnp.zeros((1, 1), I32)
    my_off = jnp.zeros((1, 1), I32)
    my_count = meta[0:1, slots : slots + 1]
    for s in range(n):
        offs.append(total)
        my_off = my_off + counts[s] * jnp.where(me > s, 1, 0)
        total = total + counts[s]

    def split(offset):
        whole = jnp.floor((offset.astype(F32) + 0.5) * (1.0 / group)).astype(I32)
        return whole, offset - whole * group

    parts = [split(offset) for offset in offs]
    my_rest = split(my_off)[1]

    def first_slot(kind, rest):
        return kind - rest + jnp.where(kind < rest, group, 0)

    def bucket_of(s, kind):
        whole, rest = parts[s]
        return whole + jnp.where(kind < rest, 1, 0), first_slot(kind, rest)

    my_pos = meta[0:1, 0:slots]
    for c in range(CHUNKS):
        entry = iota((per_chunk, slots), 0) + c * per_chunk
        slot = (entry & low) * group + first_slot(entry >> bits, my_rest)
        at = jnp.where(iota((per_chunk, slots), 1) == slot, my_pos, 0).astype(F32)
        place = jnp.sum(at, axis=1, keepdims=True)
        token = iota((per_chunk, seq_dev), 1).astype(F32)
        onehot[c * per_chunk : (c + 1) * per_chunk, :] = jnp.where(
            token == place, 1.0, 0.0
        ).astype(BF16)

    def pick(t, _):
        cols = pl.ds(pl.multiple_of(t * TILE, TILE), TILE)
        rows = jnp.dot(onehot[...], hid[:, cols], preferred_element_type=F32)
        send_rows[:, :, :, cols] = rows.astype(BF16).reshape(CHUNKS, n, bucket, TILE)
        return 0

    lax.fori_loop(0, width // TILE, pick, 0)
    for c in range(CHUNKS):
        for peer in peers:
            rows_copy(c, peer, me).start()
    for c in range(CHUNKS):
        recv_rows[c, me] = send_rows[c, me]

    def positions(c, d):
        row = iota((rows_c, slots), 0) * group + (c * n + d)
        lane = iota((rows_c, slots), 1)
        found = jnp.zeros((rows_c, slots), I32)
        for s in range(n):
            hit = (lane + offs[s] == row) & (lane < counts[s])
            found = jnp.where(hit, meta_all[s, 0:1, 0:slots] + s * seq_dev, found)
        return jnp.sum(found.astype(F32), axis=1, keepdims=True)

    lane = iota((rows_c, LANES), 1)
    half = HEAD_SIZE // 2
    freq = jnp.exp((-math.log(ROPE_BASE) * 2.0 / HEAD_SIZE) * (lane % half).astype(F32))
    turns = []
    for c in range(CHUNKS):
        angle = positions(c, me) * freq
        sine = jnp.sin(angle)
        turns.append((jnp.cos(angle), jnp.where(lane < half, -sine, sine)))
    loads[1].wait()
    for g in range(kv_local):
        vext[g, :, 0:HEAD_SIZE] = vbuf[:, g * HEAD_SIZE : (g + 1) * HEAD_SIZE]
        vext[g, :, HEAD_SIZE : 2 * HEAD_SIZE] = jnp.ones((seq_dev, HEAD_SIZE), BF16)

    def place_rows(c):
        row = iota((rows_c, per_chunk), 0)
        entry = iota((rows_c, per_chunk), 1)
        k, source = entry & low, entry >> bits
        placing = jnp.zeros((rows_c, per_chunk), F32)
        for s in range(n):
            base, first = bucket_of(s, c * n + me)
            hit = (source == s) & (row == base + k) & (k * group + first < counts[s])
            placing = jnp.where(hit, 1.0, placing)
        placing = placing.astype(BF16)
        for peer in peers:
            rows_copy(c, peer, peer).wait_recv()
        gathered = recv_rows[c].reshape(per_chunk, width)
        feats[c, hme] = jnp.dot(placing, gathered, preferred_element_type=F32).astype(BF16)
        for peer in heads:
            feat_copy(c, peer, hme).start()

    scale = 1.0 / math.sqrt(HEAD_SIZE)

    def query(c):
        for peer in heads:
            feat_copy(c, peer, peer).wait_recv()
        square = jnp.zeros((rows_c, 1), F32)
        for h in range(nh):
            wide = feats[c, h].astype(F32)
            square = square + jnp.sum(wide * wide, axis=1, keepdims=True)
        inv_rms = lax.rsqrt(square * (1.0 / (nh * width)) + EPS)
        for h in range(nh):
            gain = gain_ref[0:1, h * width : (h + 1) * width]
            normed[:, h * width : (h + 1) * width] = (
                feats[c, h].astype(F32) * inv_rms * gain
            ).astype(BF16)
        cosine, sine = turns[c]

        def project(t, _):
            cols = pl.ds(pl.multiple_of(t * TILE, TILE), TILE)
            raw = jnp.dot(normed[...], wq[:, cols], preferred_element_type=F32)
            turned = []
            for i in range(TILE // HEAD_SIZE):
                one = raw[:, i * HEAD_SIZE : (i + 1) * HEAD_SIZE]
                turned.append((one * cosine + pltpu.roll(one, half, 1) * sine) * scale)
            q_all[c, me, :, cols] = jnp.concatenate(turned, axis=1).astype(BF16)
            return 0

        lax.fori_loop(0, q_cols // TILE, project, 0)
        for peer in cores + [sibling]:
            q_copy(c, peer, me).start()

    token = (me * seq_dev + iota((1, seq_dev), 1)).astype(F32)

    def attend(c, start, stop):
        def one(step, _):
            pair = (pairs - step) % pairs
            ahead = pairs - step - 1
            both_d = [flip_bits(me, 2 * pair, n), flip_bits(me, 2 * pair + 1, n)]
            next_d = flip_bits(me, 2 * ahead, n)

            @pl.when(step == 0)
            def _():
                q_copy(c, sibling, sibling).wait_recv()

            @pl.when(step > 0)
            def _():
                q_copy(c, both_d[1], both_d[1]).wait_recv()

            def hand_on():
                @pl.when(ahead > 0)
                def _():
                    q_copy(c, next_d, next_d).wait_recv()
                    pass_copy(c, next_d).start()

            if c > 0:
                hand_on()
            pos = [positions(c, d) for d in both_d]
            bound = jnp.concatenate([pos[0]] * repeat + [pos[1]] * repeat, axis=0)
            stats = [jnp.zeros((rows_c, LANES), F32) for _ in both_d]
            for g in range(kv_local):
                rows = jnp.concatenate(
                    [
                        q_all[c, d, :, (g * repeat + i) * HEAD_SIZE : (g * repeat + i + 1) * HEAD_SIZE]
                        for d in both_d
                        for i in range(repeat)
                    ],
                    axis=0,
                )
                score = lax.dot_general(
                    rows, kbuf[:, g * HEAD_SIZE : (g + 1) * HEAD_SIZE],
                    (((1,), (1,)), ((), ())), preferred_element_type=F32,
                )
                score = jnp.where(token <= bound, score, NEG_FLOOR)
                peak = jnp.max(score, axis=1, keepdims=True)
                weight = jnp.exp(score - peak).astype(BF16)
                both = jnp.dot(weight, vext[g], preferred_element_type=F32)
                for j, d in enumerate(both_d):
                    for i in range(repeat):
                        head = g * repeat + i
                        at = (j * repeat + i) * rows_c
                        part = slice(at, at + rows_c)
                        o_send[c, d, :, head * HEAD_SIZE : (head + 1) * HEAD_SIZE] = (
                            both[part, 0:HEAD_SIZE].astype(BF16)
                        )
                        stats[j] = jnp.where(lane == head, peak[part], stats[j])
                        stats[j] = jnp.where(
                            lane == q_local + head, both[part, HEAD_SIZE:], stats[j]
                        )
            for j, d in enumerate(both_d):
                ml_send[c, d] = stats[j]

            @pl.when(step > 0)
            def _():
                o_copy(c, both_d[0], me).start()
                ml_copy(c, both_d[0], me).start()

            o_copy(c, both_d[1], me).start()
            ml_copy(c, both_d[1], me).start()
            if c == 0:
                hand_on()
            return 0

        lax.fori_loop(start, stop, one, 0)

    def join(c):
        o_recv[c, me] = o_send[c, me]
        ml_recv[c, me] = ml_send[c, me]
        for peer in peers:
            ml_copy(c, peer, peer).wait_recv()
            o_copy(c, peer, peer).wait_recv()
        top = ml_recv[c, 0]
        for s in range(1, n):
            top = jnp.maximum(top, ml_recv[c, s])
        denom = jnp.zeros((rows_c, LANES), F32)
        shares = []
        for s in range(n):
            aligned = pltpu.roll(ml_recv[c, s], LANES - q_local, 1)
            shares.append(jnp.exp(ml_recv[c, s] - top))
            denom = denom + shares[s] * aligned
        shares = [share / denom for share in shares]
        for head in range(q_local):
            cols = slice(head * HEAD_SIZE, (head + 1) * HEAD_SIZE)
            joined = jnp.zeros((rows_c, HEAD_SIZE), F32)
            for s in range(n):
                joined = joined + shares[s][:, head : head + 1] * o_recv[c, s, :, cols].astype(F32)
            mixed[:, cols] = joined.astype(BF16)
        for peer in heads + [hme]:

            def block(t, _):
                cols = pl.ds(pl.multiple_of(t * TILE, TILE), TILE)
                src = pl.ds(pl.multiple_of(peer * width + t * TILE, TILE), TILE)
                part_send[c, peer, :, cols] = jnp.dot(
                    mixed[...], wo[:, src], preferred_element_type=F32
                ).astype(BF16)
                return 0

            lax.fori_loop(0, width // TILE, block, 0)
            if peer is not hme:
                part_copy(c, peer, hme).start()
        part_recv[c, hme] = part_send[c, hme]

    def give_back(c):
        entry = iota((per_chunk, LANES), 0)
        k, source = entry & low, entry >> bits
        place = iota((per_chunk, LANES), 1)
        sending = jnp.zeros((per_chunk, LANES), F32)
        for s in range(n):
            base, first = bucket_of(s, c * n + me)
            hit = (source == s) & (place == base + k) & (k * group + first < counts[s])
            sending = jnp.where(hit, 1.0, sending)
        for peer in heads:
            part_copy(c, peer, peer).wait_recv()
        update = part_recv[c, 0].astype(F32)
        for h in range(1, nh):
            update = update + part_recv[c, h].astype(F32)
        upd[0:rows_c, :] = update.astype(BF16)
        back = jnp.dot(sending.astype(BF16), upd[...], preferred_element_type=F32)
        back_send[c] = back.astype(BF16).reshape(n, bucket, width)
        for peer in peers:
            back_copy(c, peer, me).start()
        back_recv[c, me] = back_send[c, me]

    for c in range(CHUNKS):
        place_rows(c)
    loads[2].wait()
    loads[3].wait()
    query(0)
    attend(0, 0, 1)
    query(1)
    attend(0, 1, pairs)
    query(2)
    attend(1, 0, pairs)
    loads[4].wait()
    join(0)
    attend(2, 0, pairs // 2)
    join(1)
    attend(2, pairs // 2, pairs)
    give_back(0)
    join(2)
    give_back(1)
    give_back(2)

    entry = iota((slots, entries), 1)
    source = (entry & low) * group + first_slot(entry >> bits, my_rest)
    slot = iota((slots, entries), 0)
    restoring = jnp.where((source == slot) & (slot < my_count), 1.0, 0.0).astype(BF16)
    for c in range(CHUNKS):
        for peer in peers:
            back_copy(c, peer, peer).wait_recv()
    out_ref[...] = jnp.dot(
        restoring, back_recv[...].reshape(entries, width), preferred_element_type=F32
    ).astype(BF16)

    for peer in peers:
        meta_copy(peer, me).wait_send()
    for c in range(CHUNKS):
        for peer in peers:
            rows_copy(c, peer, me).wait_send()
            o_copy(c, peer, me).wait_send()
            ml_copy(c, peer, me).wait_send()
            back_copy(c, peer, me).wait_send()
        for peer in cores + [sibling]:
            q_copy(c, peer, me).wait_send()
        for peer in cores:
            pass_copy(c, peer).wait_send()
        for peer in heads:
            feat_copy(c, peer, hme).wait_send()
            part_copy(c, peer, hme).wait_send()


def body(hidden, norm_gain, w_query, w_out, keys, values, cand_count, cand_pos):
    n, nh = lax.axis_size("seq"), lax.axis_size("head")
    seq_dev, width = hidden.shape
    slots = cand_pos.shape[0]
    bucket = -(-slots // (n * CHUNKS))
    bucket = -(-bucket // 16) * 16
    per_chunk = n * bucket
    rows_c = M_DEV // CHUNKS
    q_cols = w_query.shape[1]
    kv_local = keys.shape[1] // HEAD_SIZE
    seq_sem = pltpu.SemaphoreType.DMA((CHUNKS, n))
    head_sem = pltpu.SemaphoreType.DMA((CHUNKS, nh))
    one_sem = pltpu.SemaphoreType.DMA((n,))
    vmem, hbm = pl.BlockSpec(memory_space=pltpu.VMEM), pl.BlockSpec(memory_space=pl.ANY)
    return pl.pallas_call(
        functools.partial(kernel, n, nh, bucket),
        out_shape=jax.ShapeDtypeStruct((slots, width), BF16),
        in_specs=[vmem, vmem, hbm, vmem, hbm, hbm, hbm, hbm],
        out_specs=vmem,
        scratch_shapes=[
            pltpu.VMEM(hidden.shape, BF16),
            pltpu.VMEM(w_query.shape, BF16),
            pltpu.VMEM(w_out.shape, BF16),
            pltpu.VMEM(keys.shape, BF16),
            pltpu.VMEM(values.shape, BF16),
            pltpu.VMEM((kv_local, seq_dev, 2 * HEAD_SIZE), BF16),
            pltpu.VMEM((8, slots + LANES), I32),
            pltpu.VMEM((n, 8, slots + LANES), I32),
            pltpu.VMEM((CHUNKS * per_chunk, seq_dev), BF16),
            pltpu.VMEM((CHUNKS, n, bucket, width), BF16),
            pltpu.VMEM((CHUNKS, n, bucket, width), BF16),
            pltpu.VMEM((CHUNKS, nh, rows_c, width), BF16),
            pltpu.VMEM((rows_c, nh * width), BF16),
            pltpu.VMEM((CHUNKS, n, rows_c, q_cols), BF16),
            pltpu.VMEM((CHUNKS, n, rows_c, q_cols), BF16),
            pltpu.VMEM((CHUNKS, n, rows_c, LANES), F32),
            pltpu.VMEM((CHUNKS, n, rows_c, q_cols), BF16),
            pltpu.VMEM((CHUNKS, n, rows_c, LANES), F32),
            pltpu.VMEM((rows_c, q_cols), BF16),
            pltpu.VMEM((CHUNKS, nh, rows_c, width), BF16),
            pltpu.VMEM((CHUNKS, nh, rows_c, width), BF16),
            pltpu.VMEM((LANES, width), BF16),
            pltpu.VMEM((CHUNKS, n, bucket, width), BF16),
            pltpu.VMEM((CHUNKS, n, bucket, width), BF16),
            pltpu.SemaphoreType.DMA((5,)),
            one_sem, one_sem, seq_sem, seq_sem, head_sem, head_sem, seq_sem, seq_sem, seq_sem,
            seq_sem, seq_sem, seq_sem, seq_sem, head_sem, head_sem, seq_sem, seq_sem,
        ],
        compiler_params=pltpu.CompilerParams(
            collective_id=0, has_side_effects=True, vmem_limit_bytes=60 * 1024 * 1024
        ),
        name="routed_attention",
    )(
        cand_pos[None, :], cand_count[None, :], hidden, norm_gain[None, :],
        w_query, w_out, keys, values,
    )


def solution(mesh):
    in_specs = (
        P("seq", "head"),
        P(),
        P(None, "head"),
        P("head", None),
        P("seq", "head"),
        P("seq", "head"),
        P("seq"),
        P("seq"),
    )
    out_specs = P("seq", "head")
    return jax.shard_map(body, mesh=mesh, in_specs=in_specs, out_specs=out_specs, check_vma=False)
```

```python
import functools
import math

import jax
import jax.numpy as jnp
from jax import lax
from jax.experimental import pallas as pl
from jax.experimental.pallas import tpu as pltpu
from jax.sharding import PartitionSpec as P

HEAD_SIZE = 128
M_DEV = 96
CHUNKS = 3
LANES = 128
TILE = 256

EPS = 1e-05
ROPE_BASE = 500000.0
NEG_FLOOR = -1e30
MESH = pl.DeviceIdType.MESH
F32 = jnp.float32
BF16 = jnp.bfloat16
I32 = jnp.int32


def iota(shape, dim):
    return lax.broadcasted_iota(I32, shape, dim)


def flip_bits(index, step, count):
    out, bit = 0, 1
    while bit < count:
        out = out + bit * (((index // bit) % 2 + (step // bit) % 2) % 2)
        bit *= 2
    return out


def kernel(
    n, nh, bucket,
    pos_ref, count_ref, hidden_ref, gain_ref, wq_ref, wo_ref, key_ref, val_ref,
    out_ref,
    hid, wq, wo, kbuf, vbuf, kext, vext, pos_all,
    meta, meta_all, onehot, send_rows, recv_rows, feats, normed, q_all,
    o_send, ml_send, o_recv, ml_recv, mixed, part_send, part_recv, upd, back_send, back_recv,
    load_sem, meta_s, meta_r, rows_s, rows_r, feat_s, feat_r, q_s, q_r, pass_s,
    o_s, o_r, ml_s, ml_r, part_s, part_r, back_s, back_r,
):
    seq_dev, width = hid.shape
    slots = pos_ref.shape[0]
    kv_local = key_ref.shape[1] // HEAD_SIZE
    q_cols = wq.shape[1]
    q_local = q_cols // HEAD_SIZE
    repeat = q_local // kv_local
    group = n * CHUNKS
    rows_c = M_DEV // CHUNKS
    per_chunk = n * bucket
    entries = CHUNKS * per_chunk
    low, bits = bucket - 1, int(math.log2(bucket))
    pairs = n // 2
    me = lax.axis_index("seq")
    hme = lax.axis_index("head")

    def load(i, src, dst):
        return pltpu.make_async_copy(src, dst, load_sem.at[i])

    loads = [
        load(0, hidden_ref, hid), load(1, val_ref, vbuf), load(2, key_ref, kbuf),
        load(3, wq_ref, wq), load(4, wo_ref, wo),
    ]
    loads[0].start()

    barrier = pltpu.get_barrier_semaphore()
    for step in range(1, n):
        pl.semaphore_signal(
            barrier, inc=1, device_id=(flip_bits(me, step, n), hme), device_id_type=MESH
        )
    for step in range(1, nh):
        pl.semaphore_signal(
            barrier, inc=1, device_id=(me, (hme + step) % nh), device_id_type=MESH
        )
    meta[:, 0:slots] = jnp.broadcast_to(pos_ref[...].reshape(1, slots), (8, slots))
    meta[:, slots:] = jnp.broadcast_to(count_ref[...], (8, LANES))
    pl.semaphore_wait(barrier, n - 1 + nh - 1)

    def seq_copy(src, dst, send, recv, peer):
        return pltpu.make_async_remote_copy(
            src_ref=src, dst_ref=dst, send_sem=send, recv_sem=recv,
            device_id=(peer, hme), device_id_type=MESH,
        )

    def head_copy(src, dst, send, recv, peer):
        return pltpu.make_async_remote_copy(
            src_ref=src, dst_ref=dst, send_sem=send, recv_sem=recv,
            device_id=(me, peer), device_id_type=MESH,
        )

    def meta_copy(peer, slot):
        return seq_copy(meta, meta_all.at[slot], meta_s.at[peer], meta_r.at[slot], peer)

    def rows_copy(c, peer, slot):
        return seq_copy(
            send_rows.at[c, peer], recv_rows.at[c, slot], rows_s.at[c, peer],
            rows_r.at[c, slot], peer,
        )

    def feat_copy(c, peer, slot):
        return head_copy(
            feats.at[c, hme], feats.at[c, slot], feat_s.at[c, peer], feat_r.at[c, slot], peer
        )

    def q_copy(c, peer, slot):
        return seq_copy(
            q_all.at[c, me], q_all.at[c, slot], q_s.at[c, peer], q_r.at[c, slot], peer
        )

    def pass_copy(c, slot):
        return seq_copy(
            q_all.at[c, slot], q_all.at[c, slot], pass_s.at[c, slot], q_r.at[c, slot], sibling
        )

    def o_copy(c, peer, slot):
        return seq_copy(
            o_send.at[c, peer], o_recv.at[c, slot], o_s.at[c, peer], o_r.at[c, slot], peer
        )

    def ml_copy(c, peer, slot):
        return seq_copy(
            ml_send.at[c, peer], ml_recv.at[c, slot], ml_s.at[c, peer], ml_r.at[c, slot], peer
        )

    def part_copy(c, peer, slot):
        return head_copy(
            part_send.at[c, peer], part_recv.at[c, slot], part_s.at[c, peer],
            part_r.at[c, slot], peer,
        )

    def back_copy(c, peer, slot):
        return seq_copy(
            back_send.at[c, peer], back_recv.at[c, slot], back_s.at[c, peer],
            back_r.at[c, slot], peer,
        )

    sibling = flip_bits(me, 1, n)
    peers = [flip_bits(me, step, n) for step in range(n - 1, 0, -1)]
    cores = [flip_bits(me, step, n) for step in range(n - 2, 0, -2)]
    heads = [(hme + step) % nh for step in range(1, nh)]

    for peer in peers:
        meta_copy(peer, me).start()
    meta_all[me] = meta[...]
    loads[0].wait()
    for copy in loads[1:]:
        copy.start()
    upd[...] = jnp.zeros(upd.shape, BF16)
    for peer in peers:
        meta_copy(peer, peer).wait_recv()

    counts = [meta_all[s, 0:1, slots : slots + 1] for s in range(n)]
    offs, total = [], jnp.zeros((1, 1), I32)
    my_off = jnp.zeros((1, 1), I32)
    my_count = meta[0:1, slots : slots + 1]
    for s in range(n):
        offs.append(total)
        my_off = my_off + counts[s] * jnp.where(me > s, 1, 0)
        total = total + counts[s]

    def split(offset):
        whole = jnp.floor((offset.astype(F32) + 0.5) * (1.0 / group)).astype(I32)
        return whole, offset - whole * group

    parts = [split(offset) for offset in offs]
    my_rest = split(my_off)[1]

    def first_slot(kind, rest):
        return kind - rest + jnp.where(kind < rest, group, 0)

    def bucket_of(s, kind):
        whole, rest = parts[s]
        return whole + jnp.where(kind < rest, 1, 0), first_slot(kind, rest)

    my_pos = meta[0:1, 0:slots]
    for c in range(CHUNKS):
        entry = iota((per_chunk, slots), 0) + c * per_chunk
        slot = (entry & low) * group + first_slot(entry >> bits, my_rest)
        at = jnp.where(iota((per_chunk, slots), 1) == slot, my_pos, 0).astype(F32)
        place = jnp.sum(at, axis=1, keepdims=True)
        token = iota((per_chunk, seq_dev), 1).astype(F32)
        onehot[...] = jnp.where(token == place, 1.0, 0.0).astype(BF16)

        def pick(t, _):
            cols = pl.ds(pl.multiple_of(t * TILE, TILE), TILE)
            rows = jnp.dot(onehot[...], hid[:, cols], preferred_element_type=F32)
            send_rows[c, :, :, cols] = rows.astype(BF16).reshape(n, bucket, TILE)
            return 0

        lax.fori_loop(0, width // TILE, pick, 0)
        for peer in peers:
            rows_copy(c, peer, me).start()
        recv_rows[c, me] = send_rows[c, me]

    def positions(c, d):
        row = iota((rows_c, slots), 0) * group + (c * n + d)
        lane = iota((rows_c, slots), 1)
        found = jnp.zeros((rows_c, slots), I32)
        for s in range(n):
            hit = (lane + offs[s] == row) & (lane < counts[s])
            found = jnp.where(hit, meta_all[s, 0:1, 0:slots] + s * seq_dev, found)
        return jnp.sum(found.astype(F32), axis=1, keepdims=True)

    lane = iota((rows_c, LANES), 1)
    half = HEAD_SIZE // 2
    freq = jnp.exp((-math.log(ROPE_BASE) * 2.0 / HEAD_SIZE) * (lane % half).astype(F32))

    def note_positions(c):
        def one(d, _):
            pos_all[c, d] = jnp.broadcast_to(positions(c, d), (rows_c, LANES))
            return 0

        lax.fori_loop(0, n, one, 0)
        angle = pos_all[c, me] * freq
        sine = jnp.sin(angle)
        return jnp.cos(angle), jnp.where(lane < half, -sine, sine)

    turns = [note_positions(0)]
    loads[1].wait()
    loads[2].wait()
    for g in range(kv_local):
        kext[g] = kbuf[:, g * HEAD_SIZE : (g + 1) * HEAD_SIZE].T
        vext[g, :, 0:HEAD_SIZE] = vbuf[:, g * HEAD_SIZE : (g + 1) * HEAD_SIZE]
        vext[g, :, HEAD_SIZE : 2 * HEAD_SIZE] = jnp.ones((seq_dev, HEAD_SIZE), BF16)

    def place_rows(c):
        row = iota((rows_c, per_chunk), 0)
        entry = iota((rows_c, per_chunk), 1)
        k, source = entry & low, entry >> bits
        placing = jnp.zeros((rows_c, per_chunk), F32)
        for s in range(n):
            base, first = bucket_of(s, c * n + me)
            hit = (source == s) & (row == base + k) & (k * group + first < counts[s])
            placing = jnp.where(hit, 1.0, placing)
        placing = placing.astype(BF16)
        for peer in peers:
            rows_copy(c, peer, peer).wait_recv()
        gathered = recv_rows[c].reshape(per_chunk, width)
        feats[c, hme] = jnp.dot(placing, gathered, preferred_element_type=F32).astype(BF16)
        for peer in heads:
            feat_copy(c, peer, hme).start()

    scale = math.log2(math.e) / math.sqrt(HEAD_SIZE)

    def query(c):
        for peer in heads:
            feat_copy(c, peer, peer).wait_recv()
        square = jnp.zeros((rows_c, 1), F32)
        for h in range(nh):
            wide = feats[c, h].astype(F32)
            square = square + jnp.sum(wide * wide, axis=1, keepdims=True)
        inv_rms = lax.rsqrt(square * (1.0 / (nh * width)) + EPS)
        for h in range(nh):
            gain = gain_ref[0:1, h * width : (h + 1) * width]
            normed[:, h * width : (h + 1) * width] = (
                feats[c, h].astype(F32) * inv_rms * gain
            ).astype(BF16)
        cosine, sine = turns[c]

        def project(t, _):
            cols = pl.ds(pl.multiple_of(t * TILE, TILE), TILE)
            raw = jnp.dot(normed[...], wq[:, cols], preferred_element_type=F32)
            turned = []
            for i in range(TILE // HEAD_SIZE):
                one = raw[:, i * HEAD_SIZE : (i + 1) * HEAD_SIZE]
                turned.append((one * cosine + pltpu.roll(one, half, 1) * sine) * scale)
            q_all[c, me, :, cols] = jnp.concatenate(turned, axis=1).astype(BF16)
            return 0

        lax.fori_loop(0, q_cols // TILE, project, 0)
        for peer in cores + [sibling]:
            q_copy(c, peer, me).start()

    token = (me * seq_dev + iota((1, seq_dev), 1)).astype(F32)

    def attend(c, start, stop):
        def one(step, _):
            pair = (pairs - step) % pairs
            ahead = pairs - step - 1
            both_d = [flip_bits(me, 2 * pair, n), flip_bits(me, 2 * pair + 1, n)]
            next_d = flip_bits(me, 2 * ahead, n)

            @pl.when(step == 0)
            def _():
                q_copy(c, sibling, sibling).wait_recv()

            @pl.when(step > 0)
            def _():
                q_copy(c, both_d[1], both_d[1]).wait_recv()

            def hand_on():
                @pl.when(ahead > 0)
                def _():
                    q_copy(c, next_d, next_d).wait_recv()
                    pass_copy(c, next_d).start()

            if c > 0:
                hand_on()
            pos = [pos_all[c, d][:, 0:1] for d in both_d]
            bound = jnp.concatenate([pos[0]] * repeat + [pos[1]] * repeat, axis=0)
            stats = [jnp.zeros((rows_c, LANES), F32) for _ in both_d]
            for g in range(kv_local):
                rows = jnp.concatenate(
                    [
                        q_all[c, d, :, (g * repeat + i) * HEAD_SIZE : (g * repeat + i + 1) * HEAD_SIZE]
                        for d in both_d
                        for i in range(repeat)
                    ],
                    axis=0,
                )
                score = jnp.dot(rows, kext[g], preferred_element_type=F32)
                score = jnp.where(token <= bound, score, NEG_FLOOR)
                peak = jnp.max(score, axis=1, keepdims=True)
                weight = jnp.exp2(score - peak).astype(BF16)
                both = jnp.dot(weight, vext[g], preferred_element_type=F32)
                for j, d in enumerate(both_d):
                    for i in range(repeat):
                        head = g * repeat + i
                        at = (j * repeat + i) * rows_c
                        part = slice(at, at + rows_c)
                        o_send[c, d, :, head * HEAD_SIZE : (head + 1) * HEAD_SIZE] = (
                            both[part, 0:HEAD_SIZE].astype(BF16)
                        )
                        stats[j] = jnp.where(lane == head, peak[part], stats[j])
                        stats[j] = jnp.where(
                            lane == q_local + head, both[part, HEAD_SIZE:], stats[j]
                        )
            for j, d in enumerate(both_d):
                ml_send[c, d] = stats[j]

            @pl.when(step > 0)
            def _():
                o_copy(c, both_d[0], me).start()
                ml_copy(c, both_d[0], me).start()

            o_copy(c, both_d[1], me).start()
            ml_copy(c, both_d[1], me).start()
            if c == 0:
                hand_on()
            return 0

        lax.fori_loop(start, stop, one, 0)

    def join(c):
        o_recv[c, me] = o_send[c, me]
        ml_recv[c, me] = ml_send[c, me]
        for peer in peers:
            ml_copy(c, peer, peer).wait_recv()
            o_copy(c, peer, peer).wait_recv()
        top = ml_recv[c, 0]
        for s in range(1, n):
            top = jnp.maximum(top, ml_recv[c, s])
        denom = jnp.zeros((rows_c, LANES), F32)
        shares = []
        for s in range(n):
            aligned = pltpu.roll(ml_recv[c, s], LANES - q_local, 1)
            shares.append(jnp.exp2(ml_recv[c, s] - top))
            denom = denom + shares[s] * aligned
        shares = [share / denom for share in shares]
        for head in range(q_local):
            cols = slice(head * HEAD_SIZE, (head + 1) * HEAD_SIZE)
            joined = jnp.zeros((rows_c, HEAD_SIZE), F32)
            for s in range(n):
                joined = joined + shares[s][:, head : head + 1] * o_recv[c, s, :, cols].astype(F32)
            mixed[:, cols] = joined.astype(BF16)
        for peer in heads + [hme]:

            def block(t, _):
                cols = pl.ds(pl.multiple_of(t * TILE, TILE), TILE)
                src = pl.ds(pl.multiple_of(peer * width + t * TILE, TILE), TILE)
                part_send[c, peer, :, cols] = jnp.dot(
                    mixed[...], wo[:, src], preferred_element_type=F32
                ).astype(BF16)
                return 0

            lax.fori_loop(0, width // TILE, block, 0)
            if peer is not hme:
                part_copy(c, peer, hme).start()
        part_recv[c, hme] = part_send[c, hme]

    def give_back(c):
        entry = iota((per_chunk, LANES), 0)
        k, source = entry & low, entry >> bits
        place = iota((per_chunk, LANES), 1)
        sending = jnp.zeros((per_chunk, LANES), F32)
        for s in range(n):
            base, first = bucket_of(s, c * n + me)
            hit = (source == s) & (place == base + k) & (k * group + first < counts[s])
            sending = jnp.where(hit, 1.0, sending)
        for peer in heads:
            part_copy(c, peer, peer).wait_recv()
        update = part_recv[c, 0].astype(F32)
        for h in range(1, nh):
            update = update + part_recv[c, h].astype(F32)
        upd[0:rows_c, :] = update.astype(BF16)
        back = jnp.dot(sending.astype(BF16), upd[...], preferred_element_type=F32)
        back_send[c] = back.astype(BF16).reshape(n, bucket, width)
        for peer in peers:
            back_copy(c, peer, me).start()
        back_recv[c, me] = back_send[c, me]

    for c in range(CHUNKS):
        place_rows(c)
        if c > 0:
            turns.append(note_positions(c))
    loads[3].wait()
    query(0)
    attend(0, 0, 1)
    query(1)
    attend(0, 1, pairs)
    query(2)
    attend(1, 0, pairs)
    loads[4].wait()
    join(0)
    attend(2, 0, pairs // 2)
    join(1)
    attend(2, pairs // 2, pairs)
    give_back(0)
    join(2)
    give_back(1)
    give_back(2)

    entry = iota((slots, entries), 1)
    source = (entry & low) * group + first_slot(entry >> bits, my_rest)
    slot = iota((slots, entries), 0)
    restoring = jnp.where((source == slot) & (slot < my_count), 1.0, 0.0).astype(BF16)
    for c in range(CHUNKS):
        for peer in peers:
            back_copy(c, peer, peer).wait_recv()
    out_ref[...] = jnp.dot(
        restoring, back_recv[...].reshape(entries, width), preferred_element_type=F32
    ).astype(BF16)

    for peer in peers:
        meta_copy(peer, me).wait_send()
    for c in range(CHUNKS):
        for peer in peers:
            rows_copy(c, peer, me).wait_send()
            o_copy(c, peer, me).wait_send()
            ml_copy(c, peer, me).wait_send()
            back_copy(c, peer, me).wait_send()
        for peer in cores + [sibling]:
            q_copy(c, peer, me).wait_send()
        for peer in cores:
            pass_copy(c, peer).wait_send()
        for peer in heads:
            feat_copy(c, peer, hme).wait_send()
            part_copy(c, peer, hme).wait_send()


def body(hidden, norm_gain, w_query, w_out, keys, values, cand_count, cand_pos):
    n, nh = lax.axis_size("seq"), lax.axis_size("head")
    seq_dev, width = hidden.shape
    slots = cand_pos.shape[0]
    bucket = -(-slots // (n * CHUNKS))
    bucket = -(-bucket // 16) * 16
    per_chunk = n * bucket
    rows_c = M_DEV // CHUNKS
    q_cols = w_query.shape[1]
    kv_local = keys.shape[1] // HEAD_SIZE
    seq_sem = pltpu.SemaphoreType.DMA((CHUNKS, n))
    head_sem = pltpu.SemaphoreType.DMA((CHUNKS, nh))
    one_sem = pltpu.SemaphoreType.DMA((n,))
    vmem, hbm = pl.BlockSpec(memory_space=pltpu.VMEM), pl.BlockSpec(memory_space=pl.ANY)
    return pl.pallas_call(
        functools.partial(kernel, n, nh, bucket),
        out_shape=jax.ShapeDtypeStruct((slots, width), BF16),
        in_specs=[vmem, vmem, hbm, vmem, hbm, hbm, hbm, hbm],
        out_specs=vmem,
        scratch_shapes=[
            pltpu.VMEM(hidden.shape, BF16),
            pltpu.VMEM(w_query.shape, BF16),
            pltpu.VMEM(w_out.shape, BF16),
            pltpu.VMEM(keys.shape, BF16),
            pltpu.VMEM(values.shape, BF16),
            pltpu.VMEM((kv_local, HEAD_SIZE, seq_dev), BF16),
            pltpu.VMEM((kv_local, seq_dev, 2 * HEAD_SIZE), BF16),
            pltpu.VMEM((CHUNKS, n, rows_c, LANES), F32),
            pltpu.VMEM((8, slots + LANES), I32),
            pltpu.VMEM((n, 8, slots + LANES), I32),
            pltpu.VMEM((per_chunk, seq_dev), BF16),
            pltpu.VMEM((CHUNKS, n, bucket, width), BF16),
            pltpu.VMEM((CHUNKS, n, bucket, width), BF16),
            pltpu.VMEM((CHUNKS, nh, rows_c, width), BF16),
            pltpu.VMEM((rows_c, nh * width), BF16),
            pltpu.VMEM((CHUNKS, n, rows_c, q_cols), BF16),
            pltpu.VMEM((CHUNKS, n, rows_c, q_cols), BF16),
            pltpu.VMEM((CHUNKS, n, rows_c, LANES), F32),
            pltpu.VMEM((CHUNKS, n, rows_c, q_cols), BF16),
            pltpu.VMEM((CHUNKS, n, rows_c, LANES), F32),
            pltpu.VMEM((rows_c, q_cols), BF16),
            pltpu.VMEM((CHUNKS, nh, rows_c, width), BF16),
            pltpu.VMEM((CHUNKS, nh, rows_c, width), BF16),
            pltpu.VMEM((LANES, width), BF16),
            pltpu.VMEM((CHUNKS, n, bucket, width), BF16),
            pltpu.VMEM((CHUNKS, n, bucket, width), BF16),
            pltpu.SemaphoreType.DMA((5,)),
            one_sem, one_sem, seq_sem, seq_sem, head_sem, head_sem, seq_sem, seq_sem, seq_sem,
            seq_sem, seq_sem, seq_sem, seq_sem, head_sem, head_sem, seq_sem, seq_sem,
        ],
        compiler_params=pltpu.CompilerParams(
            collective_id=0, has_side_effects=True, vmem_limit_bytes=60 * 1024 * 1024
        ),
        name="routed_attention",
    )(
        cand_pos, cand_count[None, :], hidden, norm_gain[None, :],
        w_query, w_out, keys, values,
    )


def solution(mesh):
    in_specs = (
        P("seq", "head"),
        P(),
        P(None, "head"),
        P("head", None),
        P("seq", "head"),
        P("seq", "head"),
        P("seq"),
        P("seq"),
    )
    out_specs = P("seq", "head")
    return jax.shard_map(body, mesh=mesh, in_specs=in_specs, out_specs=out_specs, check_vma=False)
```

```python
import functools
import math

import jax
import jax.numpy as jnp
from jax import lax
from jax.experimental import pallas as pl
from jax.experimental.pallas import tpu as pltpu
from jax.sharding import PartitionSpec as P

HEAD_SIZE = 128
M_DEV = 96
CHUNKS = 3
LANES = 128
TILE = 256

EPS = 1e-05
ROPE_BASE = 500000.0
NEG_FLOOR = -1e30
MESH = pl.DeviceIdType.MESH
F32 = jnp.float32
BF16 = jnp.bfloat16
I32 = jnp.int32


def iota(shape, dim):
    return lax.broadcasted_iota(I32, shape, dim)


def flip_bits(index, step, count):
    out, bit = 0, 1
    while bit < count:
        out = out + bit * (((index // bit) % 2 + (step // bit) % 2) % 2)
        bit *= 2
    return out


def kernel(
    n, nh, bucket,
    pos_ref, count_ref, hidden_ref, gain_ref, wq_ref, wo_ref, key_ref, val_ref,
    out_ref,
    hid, wq, wo, kbuf, vbuf, kext, vext, pos_all,
    meta, meta_all, onehot, send_rows, recv_rows, feats, normed, q_all,
    o_send, ml_send, o_recv, ml_recv, mixed, part_send, part_recv, upd, back_send, back_recv,
    load_sem, meta_s, meta_r, rows_s, rows_r, feat_s, feat_r, q_s, q_r, pass_s,
    o_s, o_r, ml_s, ml_r, part_s, part_r, back_s, back_r,
):
    seq_dev, width = hid.shape
    slots = pos_ref.shape[0]
    kv_local = key_ref.shape[1] // HEAD_SIZE
    q_cols = wq.shape[1]
    q_local = q_cols // HEAD_SIZE
    repeat = q_local // kv_local
    group = n * CHUNKS
    rows_c = M_DEV // CHUNKS
    per_chunk = n * bucket
    entries = CHUNKS * per_chunk
    low, bits = bucket - 1, int(math.log2(bucket))
    pairs = n // 2
    spread = LANES * 8 // rows_c
    me = lax.axis_index("seq")
    hme = lax.axis_index("head")

    def load(i, src, dst):
        return pltpu.make_async_copy(src, dst, load_sem.at[i])

    loads = [
        load(0, hidden_ref, hid), load(1, val_ref, vbuf), load(2, key_ref, kbuf),
        load(3, wq_ref, wq), load(4, wo_ref, wo),
    ]
    loads[0].start()

    barrier = pltpu.get_barrier_semaphore()
    for step in range(1, n):
        pl.semaphore_signal(
            barrier, inc=1, device_id=(flip_bits(me, step, n), hme), device_id_type=MESH
        )
    for step in range(1, nh):
        pl.semaphore_signal(
            barrier, inc=1, device_id=(me, (hme + step) % nh), device_id_type=MESH
        )
    meta[:, 0:slots] = jnp.broadcast_to(pos_ref[...].reshape(1, slots), (8, slots))
    meta[:, slots:] = jnp.broadcast_to(count_ref[...], (8, LANES))
    pl.semaphore_wait(barrier, n - 1 + nh - 1)

    def seq_copy(src, dst, send, recv, peer):
        return pltpu.make_async_remote_copy(
            src_ref=src, dst_ref=dst, send_sem=send, recv_sem=recv,
            device_id=(peer, hme), device_id_type=MESH,
        )

    def head_copy(src, dst, send, recv, peer):
        return pltpu.make_async_remote_copy(
            src_ref=src, dst_ref=dst, send_sem=send, recv_sem=recv,
            device_id=(me, peer), device_id_type=MESH,
        )

    def meta_copy(peer, slot):
        return seq_copy(meta, meta_all.at[slot], meta_s.at[peer], meta_r.at[slot], peer)

    def rows_copy(c, peer, slot):
        return seq_copy(
            send_rows.at[c, peer], recv_rows.at[c, slot], rows_s.at[c, peer],
            rows_r.at[c, slot], peer,
        )

    def feat_copy(c, peer, slot):
        return head_copy(
            feats.at[c, hme], feats.at[c, slot], feat_s.at[c, peer], feat_r.at[c, slot], peer
        )

    def q_copy(c, peer, slot):
        return seq_copy(
            q_all.at[c, me], q_all.at[c, slot], q_s.at[c, peer], q_r.at[c, slot], peer
        )

    def pass_copy(c, slot):
        return seq_copy(
            q_all.at[c, slot], q_all.at[c, slot], pass_s.at[c, slot], q_r.at[c, slot], sibling
        )

    def o_copy(c, peer, slot):
        return seq_copy(
            o_send.at[c, peer], o_recv.at[c, slot], o_s.at[c, peer], o_r.at[c, slot], peer
        )

    def ml_copy(c, peer, slot):
        return seq_copy(
            ml_send.at[c, peer], ml_recv.at[c, slot], ml_s.at[c, peer], ml_r.at[c, slot], peer
        )

    def part_copy(c, peer, slot):
        return head_copy(
            part_send.at[c, peer], part_recv.at[c, slot], part_s.at[c, peer],
            part_r.at[c, slot], peer,
        )

    def back_copy(c, peer, slot):
        return seq_copy(
            back_send.at[c, peer], back_recv.at[c, slot], back_s.at[c, peer],
            back_r.at[c, slot], peer,
        )

    sibling = flip_bits(me, 1, n)
    peers = [flip_bits(me, step, n) for step in range(n - 1, 0, -1)]
    cores = [flip_bits(me, step, n) for step in range(n - 2, 0, -2)]
    heads = [(hme + step) % nh for step in range(1, nh)]

    for peer in peers:
        meta_copy(peer, me).start()
    meta_all[me] = meta[...]
    loads[0].wait()
    for copy in loads[1:]:
        copy.start()
    upd[...] = jnp.zeros(upd.shape, BF16)
    for peer in peers:
        meta_copy(peer, peer).wait_recv()

    counts = [meta_all[s, 0:1, slots : slots + 1] for s in range(n)]
    offs, total = [], jnp.zeros((1, 1), I32)
    my_off = jnp.zeros((1, 1), I32)
    my_count = meta[0:1, slots : slots + 1]
    for s in range(n):
        offs.append(total)
        my_off = my_off + counts[s] * jnp.where(me > s, 1, 0)
        total = total + counts[s]

    def split(offset):
        whole = jnp.floor((offset.astype(F32) + 0.5) * (1.0 / group)).astype(I32)
        return whole, offset - whole * group

    parts = [split(offset) for offset in offs]
    my_rest = split(my_off)[1]

    def first_slot(kind, rest):
        return kind - rest + jnp.where(kind < rest, group, 0)

    def bucket_of(s, kind):
        whole, rest = parts[s]
        return whole + jnp.where(kind < rest, 1, 0), first_slot(kind, rest)

    my_pos = meta[0:1, 0:slots]
    for c in range(CHUNKS):
        entry = iota((per_chunk, slots), 0) + c * per_chunk
        slot = (entry & low) * group + first_slot(entry >> bits, my_rest)
        at = jnp.where(iota((per_chunk, slots), 1) == slot, my_pos, 0).astype(F32)
        place = jnp.sum(at, axis=1, keepdims=True)
        token = iota((per_chunk, seq_dev), 1).astype(F32)
        onehot[...] = jnp.where(token == place, 1.0, 0.0).astype(BF16)

        def pick(t, _):
            cols = pl.ds(pl.multiple_of(t * TILE, TILE), TILE)
            rows = jnp.dot(onehot[...], hid[:, cols], preferred_element_type=F32)
            send_rows[c, :, :, cols] = rows.astype(BF16).reshape(n, bucket, TILE)
            return 0

        lax.fori_loop(0, width // TILE, pick, 0)
        for peer in peers:
            rows_copy(c, peer, me).start()
        recv_rows[c, me] = send_rows[c, me]

    def positions(c, d):
        row = iota((rows_c, slots), 0) * group + (c * n + d)
        lane = iota((rows_c, slots), 1)
        found = jnp.zeros((rows_c, slots), I32)
        for s in range(n):
            hit = (lane + offs[s] == row) & (lane < counts[s])
            found = jnp.where(hit, meta_all[s, 0:1, 0:slots] + s * seq_dev, found)
        return jnp.sum(found.astype(F32), axis=1, keepdims=True)

    lane = iota((rows_c, LANES), 1)
    half = HEAD_SIZE // 2
    freq = jnp.exp((-math.log(ROPE_BASE) * 2.0 / HEAD_SIZE) * (lane % half).astype(F32))

    def note_positions(c):
        def one(d, _):
            pos_all[c, d] = jnp.broadcast_to(positions(c, d), (rows_c, LANES))
            return 0

        lax.fori_loop(0, n, one, 0)
        angle = pos_all[c, me] * freq
        sine = jnp.sin(angle)
        return jnp.cos(angle), jnp.where(lane < half, -sine, sine)

    turns = [note_positions(0)]
    loads[1].wait()
    loads[2].wait()
    for g in range(kv_local):
        kext[g] = kbuf[:, g * HEAD_SIZE : (g + 1) * HEAD_SIZE].T
        vext[g, :, 0:HEAD_SIZE] = vbuf[:, g * HEAD_SIZE : (g + 1) * HEAD_SIZE]
        vext[g, :, HEAD_SIZE : 2 * HEAD_SIZE] = jnp.ones((seq_dev, HEAD_SIZE), BF16)

    def place_rows(c):
        row = iota((rows_c, per_chunk), 0)
        entry = iota((rows_c, per_chunk), 1)
        k, source = entry & low, entry >> bits
        placing = jnp.zeros((rows_c, per_chunk), F32)
        for s in range(n):
            base, first = bucket_of(s, c * n + me)
            hit = (source == s) & (row == base + k) & (k * group + first < counts[s])
            placing = jnp.where(hit, 1.0, placing)
        placing = placing.astype(BF16)
        for peer in peers:
            rows_copy(c, peer, peer).wait_recv()
        gathered = recv_rows[c].reshape(per_chunk, width)
        feats[c, hme] = jnp.dot(placing, gathered, preferred_element_type=F32).astype(BF16)
        for peer in heads:
            feat_copy(c, peer, hme).start()

    scale = math.log2(math.e) / math.sqrt(HEAD_SIZE)

    def query(c):
        for peer in heads:
            feat_copy(c, peer, peer).wait_recv()
        square = jnp.zeros((rows_c, 1), F32)
        for h in range(nh):
            wide = feats[c, h].astype(F32)
            square = square + jnp.sum(wide * wide, axis=1, keepdims=True)
        inv_rms = lax.rsqrt(square * (1.0 / (nh * width)) + EPS)
        for h in range(nh):
            gain = gain_ref[0:1, h * width : (h + 1) * width]
            normed[:, h * width : (h + 1) * width] = (
                feats[c, h].astype(F32) * inv_rms * gain
            ).astype(BF16)
        cosine, sine = turns[c]

        def project(t, _):
            cols = pl.ds(pl.multiple_of(t * TILE, TILE), TILE)
            raw = jnp.dot(normed[...], wq[:, cols], preferred_element_type=F32)
            turned = []
            for i in range(TILE // HEAD_SIZE):
                one = raw[:, i * HEAD_SIZE : (i + 1) * HEAD_SIZE]
                turned.append((one * cosine + pltpu.roll(one, half, 1) * sine) * scale)
            q_all[c, me, :, cols] = jnp.concatenate(turned, axis=1).astype(BF16)
            return 0

        lax.fori_loop(0, q_cols // TILE, project, 0)
        for peer in cores + [sibling]:
            q_copy(c, peer, me).start()

    token = (me * seq_dev + iota((1, seq_dev), 1)).astype(F32)

    def attend(c, start, stop):
        def one(step, _):
            pair = (pairs - step) % pairs
            ahead = pairs - step - 1
            both_d = [flip_bits(me, 2 * pair, n), flip_bits(me, 2 * pair + 1, n)]
            next_d = flip_bits(me, 2 * ahead, n)

            @pl.when(step == 0)
            def _():
                q_copy(c, sibling, sibling).wait_recv()

            @pl.when(step > 0)
            def _():
                q_copy(c, both_d[1], both_d[1]).wait_recv()

            def hand_on():
                @pl.when(ahead > 0)
                def _():
                    q_copy(c, next_d, next_d).wait_recv()
                    pass_copy(c, next_d).start()

            if c > 0:
                hand_on()
            pos = [pos_all[c, d][:, 0:1] for d in both_d]
            bound = jnp.concatenate([pos[0]] * repeat + [pos[1]] * repeat, axis=0)
            stats = [jnp.zeros((rows_c, LANES), F32) for _ in both_d]
            for g in range(kv_local):
                rows = jnp.concatenate(
                    [
                        q_all[c, d, :, (g * repeat + i) * HEAD_SIZE : (g * repeat + i + 1) * HEAD_SIZE]
                        for d in both_d
                        for i in range(repeat)
                    ],
                    axis=0,
                )
                score = jnp.dot(rows, kext[g], preferred_element_type=F32)
                score = jnp.where(token <= bound, score, NEG_FLOOR)
                peak = jnp.max(score, axis=1, keepdims=True)
                weight = jnp.exp2(score - peak).astype(BF16)
                both = jnp.dot(weight, vext[g], preferred_element_type=F32)
                for j, d in enumerate(both_d):
                    for i in range(repeat):
                        head = g * repeat + i
                        at = (j * repeat + i) * rows_c
                        part = slice(at, at + rows_c)
                        o_send[c, d, :, head * HEAD_SIZE : (head + 1) * HEAD_SIZE] = (
                            both[part, 0:HEAD_SIZE].astype(BF16)
                        )
                        stats[j] = jnp.where(lane == head, peak[part], stats[j])
                        stats[j] = jnp.where(
                            lane == q_local + head, both[part, HEAD_SIZE:], stats[j]
                        )
            for j, d in enumerate(both_d):
                packed = stats[j][0:8]
                for b in range(1, rows_c // 8):
                    packed = packed + pltpu.roll(stats[j][8 * b : 8 * b + 8], b * spread, 1)
                ml_send[c, d] = packed

            @pl.when(step > 0)
            def _():
                o_copy(c, both_d[0], me).start()
                ml_copy(c, both_d[0], me).start()

            o_copy(c, both_d[1], me).start()
            ml_copy(c, both_d[1], me).start()
            if c == 0:
                hand_on()
            return 0

        lax.fori_loop(start, stop, one, 0)

    def unpack(packed):
        turned = [pltpu.roll(packed, LANES - b * spread, 1) for b in range(1, rows_c // 8)]
        return jnp.concatenate([packed] + turned, axis=0)

    def join(c):
        o_recv[c, me] = o_send[c, me]
        ml_recv[c, me] = ml_send[c, me]
        for peer in peers:
            ml_copy(c, peer, peer).wait_recv()
            o_copy(c, peer, peer).wait_recv()
        stat = [unpack(ml_recv[c, s]) for s in range(n)]
        top = stat[0]
        for s in range(1, n):
            top = jnp.maximum(top, stat[s])
        denom = jnp.zeros((rows_c, LANES), F32)
        shares = []
        for s in range(n):
            aligned = pltpu.roll(stat[s], LANES - q_local, 1)
            shares.append(jnp.exp2(stat[s] - top))
            denom = denom + shares[s] * aligned
        shares = [share / denom for share in shares]
        for head in range(q_local):
            cols = slice(head * HEAD_SIZE, (head + 1) * HEAD_SIZE)
            joined = jnp.zeros((rows_c, HEAD_SIZE), F32)
            for s in range(n):
                joined = joined + shares[s][:, head : head + 1] * o_recv[c, s, :, cols].astype(F32)
            mixed[:, cols] = joined.astype(BF16)
        for peer in heads + [hme]:

            def block(t, _):
                cols = pl.ds(pl.multiple_of(t * TILE, TILE), TILE)
                src = pl.ds(pl.multiple_of(peer * width + t * TILE, TILE), TILE)
                part_send[c, peer, :, cols] = jnp.dot(
                    mixed[...], wo[:, src], preferred_element_type=F32
                ).astype(BF16)
                return 0

            lax.fori_loop(0, width // TILE, block, 0)
            if peer is not hme:
                part_copy(c, peer, hme).start()
        part_recv[c, hme] = part_send[c, hme]

    def give_back(c):
        entry = iota((per_chunk, LANES), 0)
        k, source = entry & low, entry >> bits
        place = iota((per_chunk, LANES), 1)
        sending = jnp.zeros((per_chunk, LANES), F32)
        for s in range(n):
            base, first = bucket_of(s, c * n + me)
            hit = (source == s) & (place == base + k) & (k * group + first < counts[s])
            sending = jnp.where(hit, 1.0, sending)
        for peer in heads:
            part_copy(c, peer, peer).wait_recv()
        update = part_recv[c, 0].astype(F32)
        for h in range(1, nh):
            update = update + part_recv[c, h].astype(F32)
        upd[0:rows_c, :] = update.astype(BF16)
        back = jnp.dot(sending.astype(BF16), upd[...], preferred_element_type=F32)
        back_send[c] = back.astype(BF16).reshape(n, bucket, width)
        for peer in peers:
            back_copy(c, peer, me).start()
        back_recv[c, me] = back_send[c, me]

    for c in range(CHUNKS):
        place_rows(c)
        if c > 0:
            turns.append(note_positions(c))
    loads[3].wait()
    query(0)
    attend(0, 0, 1)
    query(1)
    attend(0, 1, pairs)
    query(2)
    attend(1, 0, pairs)
    loads[4].wait()
    join(0)
    attend(2, 0, pairs // 2)
    join(1)
    attend(2, pairs // 2, pairs)
    give_back(0)
    join(2)
    give_back(1)
    give_back(2)

    entry = iota((slots, entries), 1)
    source = (entry & low) * group + first_slot(entry >> bits, my_rest)
    slot = iota((slots, entries), 0)
    restoring = jnp.where((source == slot) & (slot < my_count), 1.0, 0.0).astype(BF16)
    for c in range(CHUNKS):
        for peer in peers:
            back_copy(c, peer, peer).wait_recv()
    out_ref[...] = jnp.dot(
        restoring, back_recv[...].reshape(entries, width), preferred_element_type=F32
    ).astype(BF16)

    for peer in peers:
        meta_copy(peer, me).wait_send()
    for c in range(CHUNKS):
        for peer in peers:
            rows_copy(c, peer, me).wait_send()
            o_copy(c, peer, me).wait_send()
            ml_copy(c, peer, me).wait_send()
            back_copy(c, peer, me).wait_send()
        for peer in cores + [sibling]:
            q_copy(c, peer, me).wait_send()
        for peer in cores:
            pass_copy(c, peer).wait_send()
        for peer in heads:
            feat_copy(c, peer, hme).wait_send()
            part_copy(c, peer, hme).wait_send()


def body(hidden, norm_gain, w_query, w_out, keys, values, cand_count, cand_pos):
    n, nh = lax.axis_size("seq"), lax.axis_size("head")
    seq_dev, width = hidden.shape
    slots = cand_pos.shape[0]
    bucket = -(-slots // (n * CHUNKS))
    bucket = -(-bucket // 16) * 16
    per_chunk = n * bucket
    rows_c = M_DEV // CHUNKS
    q_cols = w_query.shape[1]
    kv_local = keys.shape[1] // HEAD_SIZE
    seq_sem = pltpu.SemaphoreType.DMA((CHUNKS, n))
    head_sem = pltpu.SemaphoreType.DMA((CHUNKS, nh))
    one_sem = pltpu.SemaphoreType.DMA((n,))
    vmem, hbm = pl.BlockSpec(memory_space=pltpu.VMEM), pl.BlockSpec(memory_space=pl.ANY)
    return pl.pallas_call(
        functools.partial(kernel, n, nh, bucket),
        out_shape=jax.ShapeDtypeStruct((slots, width), BF16),
        in_specs=[vmem, vmem, hbm, vmem, hbm, hbm, hbm, hbm],
        out_specs=vmem,
        scratch_shapes=[
            pltpu.VMEM(hidden.shape, BF16),
            pltpu.VMEM(w_query.shape, BF16),
            pltpu.VMEM(w_out.shape, BF16),
            pltpu.VMEM(keys.shape, BF16),
            pltpu.VMEM(values.shape, BF16),
            pltpu.VMEM((kv_local, HEAD_SIZE, seq_dev), BF16),
            pltpu.VMEM((kv_local, seq_dev, 2 * HEAD_SIZE), BF16),
            pltpu.VMEM((CHUNKS, n, rows_c, LANES), F32),
            pltpu.VMEM((8, slots + LANES), I32),
            pltpu.VMEM((n, 8, slots + LANES), I32),
            pltpu.VMEM((per_chunk, seq_dev), BF16),
            pltpu.VMEM((CHUNKS, n, bucket, width), BF16),
            pltpu.VMEM((CHUNKS, n, bucket, width), BF16),
            pltpu.VMEM((CHUNKS, nh, rows_c, width), BF16),
            pltpu.VMEM((rows_c, nh * width), BF16),
            pltpu.VMEM((CHUNKS, n, rows_c, q_cols), BF16),
            pltpu.VMEM((CHUNKS, n, rows_c, q_cols), BF16),
            pltpu.VMEM((CHUNKS, n, 8, LANES), F32),
            pltpu.VMEM((CHUNKS, n, rows_c, q_cols), BF16),
            pltpu.VMEM((CHUNKS, n, 8, LANES), F32),
            pltpu.VMEM((rows_c, q_cols), BF16),
            pltpu.VMEM((CHUNKS, nh, rows_c, width), BF16),
            pltpu.VMEM((CHUNKS, nh, rows_c, width), BF16),
            pltpu.VMEM((LANES, width), BF16),
            pltpu.VMEM((CHUNKS, n, bucket, width), BF16),
            pltpu.VMEM((CHUNKS, n, bucket, width), BF16),
            pltpu.SemaphoreType.DMA((5,)),
            one_sem, one_sem, seq_sem, seq_sem, head_sem, head_sem, seq_sem, seq_sem, seq_sem,
            seq_sem, seq_sem, seq_sem, seq_sem, head_sem, head_sem, seq_sem, seq_sem,
        ],
        compiler_params=pltpu.CompilerParams(
            collective_id=0, has_side_effects=True, vmem_limit_bytes=60 * 1024 * 1024
        ),
        name="routed_attention",
    )(
        cand_pos, cand_count[None, :], hidden, norm_gain[None, :],
        w_query, w_out, keys, values,
    )


def solution(mesh):
    in_specs = (
        P("seq", "head"),
        P(),
        P(None, "head"),
        P("head", None),
        P("seq", "head"),
        P("seq", "head"),
        P("seq"),
        P("seq"),
    )
    out_specs = P("seq", "head")
    return jax.shard_map(body, mesh=mesh, in_specs=in_specs, out_specs=out_specs, check_vma=False)
```
